32 devices in a mesh: rows: 4 (over y, core), chan: 8 (over z, x).
Axes of the slice: x: 2, y: 2, z: 4, core: 2. Of those that a mesh axis runs over, the one named last changes fastest.
Arguments:
- features: bfloat16 [256, 1536, 256], P('rows', 'chan'), may hold values from -6 to 6
- mixing: float32 [3, 256, 256], P(None, 'rows'), may hold values from 0 to 1, as said below
- decay_rate: float32 [256, 256], P('rows'), may hold values from 0 to 0.5, as said below
- gate_input: bfloat16 [256, 1536, 256], P('rows', 'chan'), may hold values from -6 to 6
- out_weight: bfloat16 [1536, 1536], replicated, may hold values from -0.15625 to 0.15625
Outputs:
- projected: bfloat16 [256, 1536, 256], P(('rows', 'chan'))
The draws below stay inside these ranges and needn't reach their ends.
Inputs may be any that keep to these rules, and one draw needn't show every extreme that they name: `mixing`: at every row and column the three weights are positive where their neighbour exists, the left weight is zero at column 0 and the right weight at column 255, and the three sum to one. `decay_rate`: every entry is positive.
All inputs are finite; a program needn't handle non-finite values.
Results may differ from the reference program's by a relative error of at most 0.0049.
Values may be sent and summed in bfloat16 or wider, within the bound.
A program may use at most 128 MiB of HBM per device.

```python
import jax
import jax.numpy as jnp
from jax import lax

C = 1536
STRIP_COLUMNS = 256
STRIP_ROWS = 256


def draw_mixing(key, part):
    random_keys = jax.random.split(jax.random.fold_in(key, 11), 3)
    side_low = 0.2
    side_high = 1.0
    left_w = jax.random.uniform(random_keys[0], (STRIP_ROWS, STRIP_COLUMNS), jnp.float32, side_low, side_high)
    right_w = jax.random.uniform(random_keys[1], (STRIP_ROWS, STRIP_COLUMNS), jnp.float32, side_low, side_high)
    mid_w = jax.random.uniform(random_keys[2], (STRIP_ROWS, STRIP_COLUMNS), jnp.float32, 1.0, 2.0)
    column = jnp.arange(STRIP_COLUMNS)[None, :]
    left_w = jnp.where(column == 0, 0.0, left_w)
    right_w = jnp.where(column == STRIP_COLUMNS - 1, 0.0, right_w)
    totals = left_w + mid_w + right_w
    return jnp.stack([left_w / totals, mid_w / totals, right_w / totals])


def draw_decay_rate(key, part):
    random_keys = jax.random.split(jax.random.fold_in(key, 23), 7)
    share = 0.5
    picked = jax.random.uniform(random_keys[0], (STRIP_COLUMNS,)) < share
    fast_rate = jax.random.uniform(random_keys[1], (STRIP_COLUMNS,), jnp.float32, 0.02, 0.04)
    slow_rate = jax.random.uniform(random_keys[2], (STRIP_COLUMNS,), jnp.float32, 0.05, 0.5) / STRIP_ROWS
    base_rate = jnp.where(picked, fast_rate, slow_rate)
    row_factor = jnp.exp(jax.random.uniform(random_keys[3], (STRIP_ROWS, 1), jnp.float32, -0.7, 0.7))
    cell_factor = jax.random.uniform(random_keys[4], (STRIP_ROWS, STRIP_COLUMNS), jnp.float32, 0.6, 1.4)
    decay_rates = base_rate[None, :] * row_factor * cell_factor
    spike_row_list = jax.random.randint(random_keys[5], (3,), 0, STRIP_ROWS)
    spike_event = jnp.zeros((STRIP_ROWS,), jnp.float32).at[spike_row_list].set(1.0)
    spike_frequency = jax.random.uniform(random_keys[6], (STRIP_ROWS, STRIP_COLUMNS), jnp.float32, 0.2, 0.5)
    decay_rates = jnp.where(spike_event[:, None] > 0.5, spike_frequency, decay_rates)
    return jnp.minimum(decay_rates, 0.5)


def level_of(stream_key, shape, cuts, smallest, top_value):
    gain, own = 1.0, jax.random.fold_in(stream_key, 6)
    for dim, shards_of in cuts:
        draws = jnp.exp(jax.random.uniform(jax.random.fold_in(own, dim), (shards_of,), jnp.float32, smallest / len(cuts), top_value / len(cuts)))
        gain = gain * jnp.repeat(draws, shape[dim] // shards_of).reshape([-1 if axis == dim else 1 for axis in range(len(shape))])
    return gain


def normal_values(key, dims, deviation, most, shards=(), held_as=jnp.bfloat16):
    values = jax.random.normal(key, dims, jnp.float32) * deviation
    if len(shards) > 0:
        values = level_of(key, dims, shards, -0.22, 0.18) * values
    return jnp.clip(values, min=-most, max=most).astype(held_as)


def setup_inputs(seed: int = 0) -> dict:
    key_list = jax.random.split(jax.random.key(seed), 6)
    return {
        "features": normal_values(key_list[0], (STRIP_ROWS, C, STRIP_COLUMNS), 1.0, 6.0, ((0, 4), (1, 8))),
        "mixing": draw_mixing(jax.random.fold_in(key_list[5], 71), 0),
        "decay_rate": draw_decay_rate(jax.random.fold_in(key_list[5], 71), 0),
        "gate_input": normal_values(key_list[3], (STRIP_ROWS, C, STRIP_COLUMNS), 1.0, 6.0, ((0, 4), (1, 8))),
        "out_weight": normal_values(key_list[4], (C, C), C ** -0.5, 0.15625),
    }


def reference(features, mixing, decay_rate, gate_input, out_weight):
    retain = 1.0 - decay_rate
    left_all = retain * mixing[0]
    mid_all = retain * mixing[1]
    right_all = retain * mixing[2]
    scale_all = jnp.sqrt(decay_rate)

    def advance(hidden_st, row_in):
        feat_row, gate_row, left_row, mid_row, right_row, scale_row = row_in
        edge_col = jnp.zeros((hidden_st.shape[0], 1), jnp.float32)
        before_col = jnp.concatenate([edge_col, hidden_st[:, :-1]], axis=1)
        after_col = jnp.concatenate([hidden_st[:, 1:], edge_col], axis=1)
        hidden_st = left_row[None] * before_col + mid_row[None] * hidden_st + right_row[None] * after_col
        hidden_st = hidden_st + scale_row[None] * feat_row.astype(jnp.float32)
        gated = (hidden_st * jax.nn.silu(gate_row.astype(jnp.float32))).astype(jnp.bfloat16)
        out_row = jnp.dot(out_weight, gated, preferred_element_type=jnp.float32).astype(jnp.bfloat16)
        return (hidden_st, out_row)
    start_st = jnp.zeros((features.shape[1], features.shape[2]), jnp.float32)
    _, projected = lax.scan(advance, start_st, (features, gate_input, left_all, mid_all, right_all, scale_all))
    return projected
```

```python
import functools

import jax
import jax.numpy as jnp
from jax import lax
from jax.experimental import pallas as pl
from jax.experimental.pallas import tpu as pltpu
from jax.sharding import PartitionSpec as P

MESH = pl.DeviceIdType.MESH
HIGHEST = lax.Precision.HIGHEST


def tile_of(size, choices):
    return next(t for t in choices if size % t == 0)


def partner(me, k, n):
    half = n // 2
    side, place = me // half, me % half
    across = (1 - side) * half + (place + k) % half
    beside = side * half + (place + 1 + k - half) % half
    return jnp.where(k < half, across, beside)


def kernel(n_rows, n, feat_hbm, mix_ref, decay_ref, gate_hbm, w_hbm, out_hbm,
           feat, gate, weight, coef, scale, band, ops, starts, tail, incoming, outgoing, sent, got, result,
           feat_sem, gate_sem, weight_sem, out_sem, send_sem, recv_sem, relay_send, relay_recv):
    _, chunk, ch, cols = feat.shape
    c_out = weight.shape[0]
    p, me = lax.axis_index("rows"), lax.axis_index("chan")
    tile = tile_of(ch, (64, 48, 32, 16))
    tiles = ch // tile
    o_tile = tile_of(c_out, (256, 128, 64, 32, 16))

    def feat_copy(j):
        return pltpu.make_async_copy(feat_hbm.at[j], feat.at[j], feat_sem.at[j])

    def gate_copy(j):
        return pltpu.make_async_copy(gate_hbm.at[j], gate.at[j], gate_sem.at[j])

    weight_copy = pltpu.make_async_copy(w_hbm, weight, weight_sem)

    @pl.loop(0, n)
    def _(j):
        feat_copy(j).start()

    @pl.loop(0, n)
    def _(j):
        gate_copy(j).start()

    weight_copy.start()

    barrier = pltpu.get_barrier_semaphore()

    @pl.loop(0, n - 1)
    def _(k):
        pl.semaphore_signal(barrier, inc=1, device_id={"chan": partner(me, k, n)}, device_id_type=MESH)

    @pl.when(p > 0)
    def _():
        pl.semaphore_signal(barrier, inc=1, device_id={"rows": p - 1}, device_id_type=MESH)

    @pl.when(p < n_rows - 1)
    def _():
        pl.semaphore_signal(barrier, inc=1, device_id={"rows": p + 1}, device_id_type=MESH)

    retain = 1.0 - decay_ref[...]
    for s in range(3):
        coef[s] = retain * mix_ref[s]
    scale[...] = jnp.sqrt(decay_ref[...])

    def step(state, j, row):
        left_w = coef[0, j, pl.ds(row, 1), :]
        mid_w = coef[1, j, pl.ds(row, 1), :]
        right_w = coef[2, j, pl.ds(row, 1), :]
        return left_w * pltpu.roll(state, 1, 1) + mid_w * state + right_w * pltpu.roll(state, cols - 1, 1)

    def advance(state, j, row, at):
        push = scale[j, pl.ds(row, 1), :] * feat[j, row, at, :].astype(jnp.float32)
        return step(state, j, row) + push

    tail[...] = jnp.zeros_like(tail)

    @pl.loop(0, n)
    def _(j):
        feat_copy(j).wait()

        @pl.loop(0, tiles)
        def _(t):
            at = pl.ds(pl.multiple_of(t * tile, tile), tile)
            state = tail[at, :]
            starts[j, at, :] = state
            for row in range(chunk):
                state = advance(state, j, row, at)
            tail[at, :] = state

    @pl.when(p > 0)
    def _():
        depth = band.shape[1]
        diagonal = lax.broadcasted_iota(jnp.int32, band.shape, 1)
        value = jnp.where(diagonal == chunk, 1.0, 0.0).astype(jnp.float32)
        for row in range(chunk):
            below = pltpu.roll(pltpu.roll(value, depth - 1, 1), 1, 2)
            above = pltpu.roll(pltpu.roll(value, 1, 1), cols - 1, 2)
            value = (coef[0, :, row:row + 1, :] * below + coef[1, :, row:row + 1, :] * value
                     + coef[2, :, row:row + 1, :] * above)
        band[...] = value
        offset = (lax.broadcasted_iota(jnp.int32, (cols, cols), 0)
                  - lax.broadcasted_iota(jnp.int32, (cols, cols), 1))
        ops[0] = jnp.where(offset == 0, 1.0, 0.0).astype(jnp.float32)

        @pl.loop(0, n)
        def _(j):
            dense = jnp.zeros((cols, cols), jnp.float32)
            for k in range(2 * chunk + 1):
                dense = jnp.where(offset == k - chunk, band[j, k:k + 1, :], dense)
            ops[j + 1] = jnp.dot(ops[j], dense, precision=HIGHEST, preferred_element_type=jnp.float32)

    pl.semaphore_wait(barrier, n - 1 + jnp.where(p > 0, 1, 0) + jnp.where(p < n_rows - 1, 1, 0))

    def relay(device):
        return pltpu.make_async_remote_copy(
            src_ref=outgoing, dst_ref=incoming, send_sem=relay_send, recv_sem=relay_recv,
            device_id={"rows": device}, device_id_type=MESH)

    @pl.when(p > 0)
    def _():
        relay(p - 1).wait_recv()

    @pl.when(p < n_rows - 1)
    def _():
        @pl.when(p == 0)
        def _():
            outgoing[...] = tail[...]

        @pl.when(p > 0)
        def _():
            outgoing[...] = tail[...] + jnp.dot(
                incoming[...], ops[n], precision=HIGHEST, preferred_element_type=jnp.float32)

        relay(p + 1).start()

    def send(row, k):
        return pltpu.make_async_remote_copy(
            src_ref=sent.at[k, row], dst_ref=got.at[row, pl.ds(pl.multiple_of(me * ch, ch), ch), :],
            send_sem=send_sem.at[row, k], recv_sem=recv_sem.at[row, k],
            device_id={"chan": partner(me, k, n)}, device_id_type=MESH)

    def gated_row(j, row, put):
        @pl.loop(0, tiles)
        def _(t):
            at = pl.ds(pl.multiple_of(t * tile, tile), tile)
            state = advance(starts[j, at, :], j, row, at)
            starts[j, at, :] = state
            v = gate[j, row, at, :].astype(jnp.float32)
            put(t, (state * (v / (1.0 + jnp.exp(-v)))).astype(jnp.bfloat16))

    @pl.loop(0, chunk)
    def _(row):
        @pl.loop(0, n)
        def _(k):
            j = partner(me, k, n)

            @pl.when(row == 0)
            def _():
                gate_copy(j).wait()

                @pl.when(p > 0)
                def _():
                    starts[j] = starts[j] + jnp.dot(
                        incoming[...], ops[j], precision=HIGHEST, preferred_element_type=jnp.float32)

            @pl.when(k < n - 1)
            def _():
                def put(t, value):
                    sent[k, row, pl.ds(pl.multiple_of(t * tile, tile), tile), :] = value

                gated_row(j, row, put)
                send(row, k).start()

            @pl.when(k == n - 1)
            def _():
                def put(t, value):
                    got[row, pl.ds(pl.multiple_of(me * ch + t * tile, tile), tile), :] = value

                gated_row(j, row, put)

    weight_copy.wait()

    def out_copy(row):
        return pltpu.make_async_copy(result.at[row], out_hbm.at[row], out_sem.at[row])

    @pl.loop(0, chunk)
    def _(row):
        @pl.loop(0, n - 1)
        def _(k):
            send(row, k).wait_recv()

        @pl.loop(0, c_out // o_tile)
        def _(o):
            at = pl.ds(pl.multiple_of(o * o_tile, o_tile), o_tile)
            result[row, at, :] = jnp.dot(
                weight[at, :], got[row], preferred_element_type=jnp.float32).astype(jnp.bfloat16)

        out_copy(row).start()

    @pl.loop(0, chunk)
    def _(row):
        @pl.loop(0, n - 1)
        def _(k):
            send(row, k).wait_send()

        out_copy(row).wait()

    @pl.when(p < n_rows - 1)
    def _():
        relay(p + 1).wait_send()


def shards(n_rows, n, features, mixing, decay_rate, gate_input, out_weight):
    rows_here, ch, cols = features.shape
    chunk = rows_here // n
    c_out, c_in = out_weight.shape
    depth = -(-(2 * chunk + 1) // 8) * 8
    f32, bf16 = jnp.float32, jnp.bfloat16
    any_spec = pl.BlockSpec(memory_space=pl.ANY)
    vmem_spec = pl.BlockSpec(memory_space=pltpu.VMEM)
    dma = pltpu.SemaphoreType.DMA
    flops = 2 * chunk * c_out * c_in * cols
    return pl.pallas_call(
        functools.partial(kernel, n_rows, n),
        out_shape=jax.ShapeDtypeStruct((chunk, c_out, cols), bf16),
        in_specs=[any_spec, vmem_spec, vmem_spec, any_spec, any_spec],
        out_specs=any_spec,
        scratch_shapes=[
            pltpu.VMEM((n, chunk, ch, cols), bf16),
            pltpu.VMEM((n, chunk, ch, cols), bf16),
            pltpu.VMEM((c_out, c_in), bf16),
            pltpu.VMEM((3, n, chunk, cols), f32),
            pltpu.VMEM((n, chunk, cols), f32),
            pltpu.VMEM((n, depth, cols), f32),
            pltpu.VMEM((n + 1, cols, cols), f32),
            pltpu.VMEM((n, ch, cols), f32),
            pltpu.VMEM((ch, cols), f32),
            pltpu.VMEM((ch, cols), f32),
            pltpu.VMEM((ch, cols), f32),
            pltpu.VMEM((n, chunk, ch, cols), bf16),
            pltpu.VMEM((chunk, c_in, cols), bf16),
            pltpu.VMEM((chunk, c_out, cols), bf16),
            dma((n,)),
            dma((n,)),
            dma,
            dma((chunk,)),
            dma((chunk, n)),
            dma((chunk, n)),
            dma,
            dma,
        ],
        compiler_params=pltpu.CompilerParams(
            collective_id=0, has_side_effects=True, vmem_limit_bytes=58 * 2**20),
        cost_estimate=pl.CostEstimate(flops=flops, bytes_accessed=4 * features.size * 2, transcendentals=features.size),
    )(
        features.reshape(n, chunk, ch, cols),
        mixing.reshape(3, n, chunk, cols),
        decay_rate.reshape(n, chunk, cols),
        gate_input.reshape(n, chunk, ch, cols),
        out_weight,
    )


def solution(mesh):
    n_rows, n = mesh.shape["rows"], mesh.shape["chan"]
    in_specs = (
        P("rows", "chan", None),
        P(None, "rows", None),
        P("rows", None),
        P("rows", "chan", None),
        P(),
    )
    out_specs = P(("rows", "chan"), None, None)
    return jax.shard_map(
        functools.partial(shards, n_rows, n), mesh=mesh, in_specs=in_specs, out_specs=out_specs, check_vma=False)
```

```python
import functools

import jax
import jax.numpy as jnp
from jax import lax
from jax.experimental import pallas as pl
from jax.experimental.pallas import tpu as pltpu
from jax.sharding import PartitionSpec as P

MESH = pl.DeviceIdType.MESH


def tile_of(size, choices):
    return next(t for t in choices if size % t == 0)


def halves(value):
    high = value.astype(jnp.bfloat16)
    return high, (value - high.astype(jnp.float32)).astype(jnp.bfloat16)


def dot3(a_hi, a_lo, b_hi, b_lo):
    dot = functools.partial(jnp.dot, preferred_element_type=jnp.float32)
    return dot(a_hi, b_hi) + (dot(a_hi, b_lo) + dot(a_lo, b_hi))


def partner(me, k, n):
    half = n // 2
    side, place = me // half, me % half
    across = (1 - side) * half + (place + k) % half
    beside = side * half + (place + 1 + k - half) % half
    return jnp.where(k < half, across, beside)


def kernel(n_rows, n, feat_hbm, mix_ref, decay_ref, gate_hbm, w_hbm, out_hbm,
           feat, gate, weight, coef, scale, band, ops_hi, ops_lo, starts, tail,
           incoming, outgoing, come_hi, come_lo, sent, got, result,
           feat_sem, gate_sem, weight_sem, out_sem, send_sem, recv_sem, relay_send, relay_recv):
    _, chunk, ch, cols = feat.shape
    c_out = weight.shape[0]
    p, me = lax.axis_index("rows"), lax.axis_index("chan")
    tile = tile_of(ch, (64, 48, 32, 16))
    tiles = ch // tile
    o_tile = tile_of(c_out, (256, 128, 64, 32, 16))

    def feat_copy(j):
        return pltpu.make_async_copy(feat_hbm.at[j], feat.at[j], feat_sem.at[j])

    def gate_copy(j):
        return pltpu.make_async_copy(gate_hbm.at[j], gate.at[j], gate_sem.at[j])

    weight_copy = pltpu.make_async_copy(w_hbm, weight, weight_sem)

    @pl.loop(0, n)
    def _(j):
        feat_copy(j).start()

    @pl.loop(0, n)
    def _(j):
        gate_copy(j).start()

    weight_copy.start()

    barrier = pltpu.get_barrier_semaphore()

    @pl.loop(0, n - 1)
    def _(k):
        pl.semaphore_signal(barrier, inc=1, device_id={"chan": partner(me, k, n)}, device_id_type=MESH)

    @pl.when(p > 0)
    def _():
        pl.semaphore_signal(barrier, inc=1, device_id={"rows": p - 1}, device_id_type=MESH)

    @pl.when(p < n_rows - 1)
    def _():
        pl.semaphore_signal(barrier, inc=1, device_id={"rows": p + 1}, device_id_type=MESH)

    retain = 1.0 - decay_ref[...]
    for s in range(3):
        coef[s] = retain * mix_ref[s]
    scale[...] = jnp.sqrt(decay_ref[...])

    def step(state, j, row):
        left_w = coef[0, j, pl.ds(row, 1), :]
        mid_w = coef[1, j, pl.ds(row, 1), :]
        right_w = coef[2, j, pl.ds(row, 1), :]
        return left_w * pltpu.roll(state, 1, 1) + mid_w * state + right_w * pltpu.roll(state, cols - 1, 1)

    def advance(state, j, row, at):
        push = scale[j, pl.ds(row, 1), :] * feat[j, row, at, :].astype(jnp.float32)
        return step(state, j, row) + push

    def scan_tile(j, t):
        at = pl.ds(t * tile, tile)
        state = tail[at, :]
        starts[j, at, :] = state
        for row in range(chunk):
            state = advance(state, j, row, at)
        tail[at, :] = state

    tail[...] = jnp.zeros_like(tail)

    @pl.when(p == 0)
    def _():
        @pl.loop(0, n)
        def _(j):
            feat_copy(j).wait()
            for t in range(tiles):
                scan_tile(j, t)

    @pl.when(p > 0)
    def _():
        depth = band.shape[1]
        diagonal = lax.broadcasted_iota(jnp.int32, band.shape, 1)
        value = jnp.where(diagonal == chunk, 1.0, 0.0).astype(jnp.float32)
        for row in range(chunk):
            below = pltpu.roll(pltpu.roll(value, depth - 1, 1), 1, 2)
            above = pltpu.roll(pltpu.roll(value, 1, 1), cols - 1, 2)
            value = (coef[0, :, row:row + 1, :] * below + coef[1, :, row:row + 1, :] * value
                     + coef[2, :, row:row + 1, :] * above)
        band[...] = value
        offset = (lax.broadcasted_iota(jnp.int32, (cols, cols), 0)
                  - lax.broadcasted_iota(jnp.int32, (cols, cols), 1))
        ops_hi[0] = jnp.where(offset == 0, 1.0, 0.0).astype(jnp.bfloat16)
        ops_lo[0] = jnp.zeros((cols, cols), jnp.bfloat16)

        @pl.loop(0, n)
        def _(j):
            feat_copy(j).wait()
            dense = jnp.zeros((cols, cols), jnp.float32)
            for k in range(2 * chunk + 1):
                dense = jnp.where(offset == k - chunk, band[j, k:k + 1, :], dense)
            product = dot3(ops_hi[j], ops_lo[j], *halves(dense))
            ops_hi[j + 1], ops_lo[j + 1] = halves(product)
            for t in range(tiles):
                scan_tile(j, t)

    pl.semaphore_wait(barrier, n - 1 + jnp.where(p > 0, 1, 0) + jnp.where(p < n_rows - 1, 1, 0))

    def relay(device, t):
        at = pl.ds(t * tile, tile)
        return pltpu.make_async_remote_copy(
            src_ref=outgoing.at[at, :], dst_ref=incoming.at[at, :],
            send_sem=relay_send.at[t], recv_sem=relay_recv.at[t],
            device_id={"rows": device}, device_id_type=MESH)

    for t in range(tiles):
        at = pl.ds(t * tile, tile)

        @pl.when(p > 0)
        def _():
            relay(p - 1, t).wait_recv()
            come_hi[at, :], come_lo[at, :] = halves(incoming[at, :])

        @pl.when(p < n_rows - 1)
        def _():
            @pl.when(p == 0)
            def _():
                outgoing[at, :] = tail[at, :]

            @pl.when(p > 0)
            def _():
                outgoing[at, :] = tail[at, :] + dot3(come_hi[at, :], come_lo[at, :], ops_hi[n], ops_lo[n])

            relay(p + 1, t).start()

    def send(row, k):
        return pltpu.make_async_remote_copy(
            src_ref=sent.at[k, row], dst_ref=got.at[row, pl.ds(pl.multiple_of(me * ch, ch), ch), :],
            send_sem=send_sem.at[row, k], recv_sem=recv_sem.at[row, k],
            device_id={"chan": partner(me, k, n)}, device_id_type=MESH)

    def gated_row(j, row, put):
        @pl.loop(0, tiles)
        def _(t):
            at = pl.ds(pl.multiple_of(t * tile, tile), tile)
            state = advance(starts[j, at, :], j, row, at)
            starts[j, at, :] = state
            v = gate[j, row, at, :].astype(jnp.float32)
            put(t, (state * (v / (1.0 + jnp.exp(-v)))).astype(jnp.bfloat16))

    @pl.loop(0, chunk)
    def _(row):
        @pl.loop(0, n)
        def _(k):
            j = partner(me, k, n)

            @pl.when(row == 0)
            def _():
                gate_copy(j).wait()

                @pl.when(p > 0)
                def _():
                    starts[j] = starts[j] + dot3(come_hi[...], come_lo[...], ops_hi[j], ops_lo[j])

            @pl.when(k < n - 1)
            def _():
                def put(t, value):
                    sent[k, row, pl.ds(pl.multiple_of(t * tile, tile), tile), :] = value

                gated_row(j, row, put)
                send(row, k).start()

            @pl.when(k == n - 1)
            def _():
                def put(t, value):
                    got[row, pl.ds(pl.multiple_of(me * ch + t * tile, tile), tile), :] = value

                gated_row(j, row, put)

    weight_copy.wait()

    def out_copy(row):
        return pltpu.make_async_copy(result.at[row], out_hbm.at[row], out_sem.at[row])

    @pl.loop(0, chunk)
    def _(row):
        @pl.loop(0, n - 1)
        def _(k):
            send(row, k).wait_recv()

        @pl.loop(0, c_out // o_tile)
        def _(o):
            at = pl.ds(pl.multiple_of(o * o_tile, o_tile), o_tile)
            result[row, at, :] = jnp.dot(
                weight[at, :], got[row], preferred_element_type=jnp.float32).astype(jnp.bfloat16)

        out_copy(row).start()

    @pl.loop(0, chunk)
    def _(row):
        @pl.loop(0, n - 1)
        def _(k):
            send(row, k).wait_send()

        out_copy(row).wait()

    @pl.when(p < n_rows - 1)
    def _():
        for t in range(tiles):
            relay(p + 1, t).wait_send()


def copy_kernel(source, target, sem):
    copies = [pltpu.make_async_copy(source.at[i], target.at[i], sem.at[i]) for i in range(source.shape[0])]
    for copy in copies:
        copy.start()
    for copy in copies:
        copy.wait()


def shards(n_rows, n, features, mixing, decay_rate, gate_input, out_weight):
    rows_here, ch, cols = features.shape
    chunk = rows_here // n
    c_out, c_in = out_weight.shape
    tiles = ch // tile_of(ch, (64, 48, 32, 16))
    depth = -(-(2 * chunk + 1) // 8) * 8
    f32, bf16 = jnp.float32, jnp.bfloat16
    any_spec = pl.BlockSpec(memory_space=pl.ANY)
    vmem_spec = pl.BlockSpec(memory_space=pltpu.VMEM)
    dma = pltpu.SemaphoreType.DMA
    flops = 2 * chunk * c_out * c_in * cols
    projected = pl.pallas_call(
        functools.partial(kernel, n_rows, n),
        out_shape=jax.ShapeDtypeStruct((chunk, c_out, cols), bf16),
        in_specs=[any_spec, vmem_spec, vmem_spec, any_spec, any_spec],
        out_specs=any_spec,
        scratch_shapes=[
            pltpu.VMEM((n, chunk, ch, cols), bf16),
            pltpu.VMEM((n, chunk, ch, cols), bf16),
            pltpu.VMEM((c_out, c_in), bf16),
            pltpu.VMEM((3, n, chunk, cols), f32),
            pltpu.VMEM((n, chunk, cols), f32),
            pltpu.VMEM((n, depth, cols), f32),
            pltpu.VMEM((n + 1, cols, cols), bf16),
            pltpu.VMEM((n + 1, cols, cols), bf16),
            pltpu.VMEM((n, ch, cols), f32),
            pltpu.VMEM((ch, cols), f32),
            pltpu.VMEM((ch, cols), f32),
            pltpu.VMEM((ch, cols), f32),
            pltpu.VMEM((ch, cols), bf16),
            pltpu.VMEM((ch, cols), bf16),
            pltpu.VMEM((n, chunk, ch, cols), bf16),
            pltpu.VMEM((chunk, c_in, cols), bf16),
            pltpu.VMEM((chunk, c_out, cols), bf16),
            dma((n,)),
            dma((n,)),
            dma,
            dma((chunk,)),
            dma((chunk, n)),
            dma((chunk, n)),
            dma((tiles,)),
            dma((tiles,)),
        ],
        compiler_params=pltpu.CompilerParams(
            collective_id=0, has_side_effects=True, vmem_limit_bytes=58 * 2**20),
        cost_estimate=pl.CostEstimate(flops=flops, bytes_accessed=4 * features.size * 2, transcendentals=features.size),
    )(
        features.reshape(n, chunk, ch, cols),
        mixing.reshape(3, n, chunk, cols),
        decay_rate.reshape(n, chunk, cols),
        gate_input.reshape(n, chunk, ch, cols),
        out_weight,
    )
    return pl.pallas_call(
        copy_kernel,
        out_shape=jax.ShapeDtypeStruct(projected.shape, bf16),
        in_specs=[any_spec],
        out_specs=any_spec,
        scratch_shapes=[dma((chunk,))],
    )(projected)


def solution(mesh):
    n_rows, n = mesh.shape["rows"], mesh.shape["chan"]
    in_specs = (
        P("rows", "chan", None),
        P(None, "rows", None),
        P("rows", None),
        P("rows", "chan", None),
        P(),
    )
    out_specs = P(("rows", "chan"), None, None)
    return jax.shard_map(
        functools.partial(shards, n_rows, n), mesh=mesh, in_specs=in_specs, out_specs=out_specs, check_vma=False)
```

```python
import functools

import jax
import jax.numpy as jnp
from jax import lax
from jax.experimental import pallas as pl
from jax.experimental.pallas import tpu as pltpu
from jax.sharding import PartitionSpec as P

MESH = pl.DeviceIdType.MESH


def tile_of(size, choices):
    return next(t for t in choices if size % t == 0)


def halves(value):
    high = value.astype(jnp.bfloat16)
    return high, (value - high.astype(jnp.float32)).astype(jnp.bfloat16)


def dot3(a_hi, a_lo, b_hi, b_lo):
    dot = functools.partial(jnp.dot, preferred_element_type=jnp.float32)
    return dot(a_hi, b_hi) + (dot(a_hi, b_lo) + dot(a_lo, b_hi))


def partner(me, k, n):
    half = n // 2
    mask = jnp.where(k < half, n - 1 - k, (k - half + 1) % half)
    result, bit = 0, 1
    while bit < n:
        result += (me // bit + mask // bit) % 2 * bit
        bit *= 2
    return result


def kernel(n_rows, n, feat_hbm, mix_ref, decay_ref, gate_hbm, w_hbm, out_hbm,
           feat, gate, weight, coef, scale, band, ops_hi, ops_lo, starts, tail,
           incoming, outgoing, come_hi, come_lo, sent, got, result,
           feat_sem, gate_sem, weight_sem, out_sem, send_sem, recv_sem, relay_send, relay_recv):
    _, chunk, ch, cols = feat.shape
    c_out = weight.shape[0]
    p, me = lax.axis_index("rows"), lax.axis_index("chan")
    tile = tile_of(ch, (64, 48, 32, 16))
    tiles = ch // tile
    o_tile = tile_of(c_out, (256, 128, 64, 32, 16))

    def feat_copy(j):
        return pltpu.make_async_copy(feat_hbm.at[j], feat.at[j], feat_sem.at[j])

    def gate_copy(j):
        return pltpu.make_async_copy(gate_hbm.at[j], gate.at[j], gate_sem.at[j])

    weight_copy = pltpu.make_async_copy(w_hbm, weight, weight_sem)

    @pl.loop(0, n)
    def _(j):
        feat_copy(j).start()

    @pl.loop(0, n)
    def _(j):
        gate_copy(j).start()

    weight_copy.start()

    barrier = pltpu.get_barrier_semaphore()

    @pl.loop(0, n - 1)
    def _(k):
        pl.semaphore_signal(barrier, inc=1, device_id={"chan": partner(me, k, n)}, device_id_type=MESH)

    @pl.when(p > 0)
    def _():
        pl.semaphore_signal(barrier, inc=1, device_id={"rows": p - 1}, device_id_type=MESH)

    @pl.when(p < n_rows - 1)
    def _():
        pl.semaphore_signal(barrier, inc=1, device_id={"rows": p + 1}, device_id_type=MESH)

    retain = 1.0 - decay_ref[...]
    for s in range(3):
        coef[s] = retain * mix_ref[s]
    scale[...] = jnp.sqrt(decay_ref[...])

    def step(state, j, row):
        left_w = coef[0, j, pl.ds(row, 1), :]
        mid_w = coef[1, j, pl.ds(row, 1), :]
        right_w = coef[2, j, pl.ds(row, 1), :]
        return left_w * pltpu.roll(state, 1, 1) + mid_w * state + right_w * pltpu.roll(state, cols - 1, 1)

    def advance(state, j, row, at):
        push = scale[j, pl.ds(row, 1), :] * feat[j, row, at, :].astype(jnp.float32)
        return step(state, j, row) + push

    def scan_tile(j, t):
        at = pl.ds(t * tile, tile)
        state = tail[at, :]
        starts[j, at, :] = state
        for row in range(chunk):
            state = advance(state, j, row, at)
        tail[at, :] = state

    tail[...] = jnp.zeros_like(tail)

    @pl.when(p == 0)
    def _():
        @pl.loop(0, n)
        def _(j):
            feat_copy(j).wait()
            for t in range(tiles):
                scan_tile(j, t)

    @pl.when(p > 0)
    def _():
        depth = band.shape[1]
        diagonal = lax.broadcasted_iota(jnp.int32, band.shape, 1)
        value = jnp.where(diagonal == chunk, 1.0, 0.0).astype(jnp.float32)
        for row in range(chunk):
            below = pltpu.roll(pltpu.roll(value, depth - 1, 1), 1, 2)
            above = pltpu.roll(pltpu.roll(value, 1, 1), cols - 1, 2)
            value = (coef[0, :, row:row + 1, :] * below + coef[1, :, row:row + 1, :] * value
                     + coef[2, :, row:row + 1, :] * above)
        band[...] = value
        offset = (lax.broadcasted_iota(jnp.int32, (cols, cols), 0)
                  - lax.broadcasted_iota(jnp.int32, (cols, cols), 1))
        ops_hi[0] = jnp.where(offset == 0, 1.0, 0.0).astype(jnp.bfloat16)
        ops_lo[0] = jnp.zeros((cols, cols), jnp.bfloat16)

        @pl.loop(0, n)
        def _(j):
            feat_copy(j).wait()
            dense = jnp.zeros((cols, cols), jnp.float32)
            for k in range(2 * chunk + 1):
                dense = jnp.where(offset == k - chunk, band[j, k:k + 1, :], dense)
            product = dot3(ops_hi[j], ops_lo[j], *halves(dense))
            ops_hi[j + 1], ops_lo[j + 1] = halves(product)
            for t in range(tiles):
                scan_tile(j, t)

    pl.semaphore_wait(barrier, n - 1 + jnp.where(p > 0, 1, 0) + jnp.where(p < n_rows - 1, 1, 0))

    def relay(device, t):
        at = pl.ds(t * tile, tile)
        return pltpu.make_async_remote_copy(
            src_ref=outgoing.at[at, :], dst_ref=incoming.at[at, :],
            send_sem=relay_send.at[t], recv_sem=relay_recv.at[t],
            device_id={"rows": device}, device_id_type=MESH)

    for t in range(tiles):
        at = pl.ds(t * tile, tile)

        @pl.when(p > 0)
        def _():
            relay(p - 1, t).wait_recv()
            come_hi[at, :], come_lo[at, :] = halves(incoming[at, :])

        @pl.when(p < n_rows - 1)
        def _():
            @pl.when(p == 0)
            def _():
                outgoing[at, :] = tail[at, :]

            @pl.when(p > 0)
            def _():
                outgoing[at, :] = tail[at, :] + dot3(come_hi[at, :], come_lo[at, :], ops_hi[n], ops_lo[n])

            relay(p + 1, t).start()

    def send(row, k):
        return pltpu.make_async_remote_copy(
            src_ref=sent.at[k, row], dst_ref=got.at[row, pl.ds(pl.multiple_of(me * ch, ch), ch), :],
            send_sem=send_sem.at[row, k], recv_sem=recv_sem.at[row, k],
            device_id={"chan": partner(me, k, n)}, device_id_type=MESH)

    def gated_row(j, row, put):
        @pl.loop(0, tiles)
        def _(t):
            at = pl.ds(pl.multiple_of(t * tile, tile), tile)
            state = advance(starts[j, at, :], j, row, at)
            starts[j, at, :] = state
            v = gate[j, row, at, :].astype(jnp.float32)
            put(t, (state * (v / (1.0 + jnp.exp(-v)))).astype(jnp.bfloat16))

    @pl.loop(0, chunk)
    def _(row):
        @pl.loop(0, n)
        def _(k):
            j = partner(me, k, n)

            @pl.when(row == 0)
            def _():
                gate_copy(j).wait()

                @pl.when(p > 0)
                def _():
                    starts[j] = starts[j] + dot3(come_hi[...], come_lo[...], ops_hi[j], ops_lo[j])

            @pl.when(k < n - 1)
            def _():
                def put(t, value):
                    sent[k, row, pl.ds(pl.multiple_of(t * tile, tile), tile), :] = value

                gated_row(j, row, put)
                send(row, k).start()

            @pl.when(k == n - 1)
            def _():
                def put(t, value):
                    got[row, pl.ds(pl.multiple_of(me * ch + t * tile, tile), tile), :] = value

                gated_row(j, row, put)

    weight_copy.wait()

    def out_copy(row):
        return pltpu.make_async_copy(result.at[row], out_hbm.at[row], out_sem.at[row])

    @pl.loop(0, chunk)
    def _(row):
        @pl.loop(0, n - 1)
        def _(k):
            send(row, k).wait_recv()

        @pl.loop(0, c_out // o_tile)
        def _(o):
            at = pl.ds(pl.multiple_of(o * o_tile, o_tile), o_tile)
            result[row, at, :] = jnp.dot(
                weight[at, :], got[row], preferred_element_type=jnp.float32).astype(jnp.bfloat16)

        out_copy(row).start()

    @pl.loop(0, chunk)
    def _(row):
        @pl.loop(0, n - 1)
        def _(k):
            send(row, k).wait_send()

        out_copy(row).wait()

    @pl.when(p < n_rows - 1)
    def _():
        for t in range(tiles):
            relay(p + 1, t).wait_send()


def copy_kernel(source, target, held, in_sem, out_sem):
    rows = range(source.shape[0])
    ins = [pltpu.make_async_copy(source.at[i], held.at[i], in_sem.at[i]) for i in rows]
    outs = [pltpu.make_async_copy(held.at[i], target.at[i], out_sem.at[i]) for i in rows]
    for copy in ins:
        copy.start()
    for i in rows:
        ins[i].wait()
        outs[i].start()
    for copy in outs:
        copy.wait()


def shards(n_rows, n, features, mixing, decay_rate, gate_input, out_weight):
    rows_here, ch, cols = features.shape
    chunk = rows_here // n
    c_out, c_in = out_weight.shape
    tiles = ch // tile_of(ch, (64, 48, 32, 16))
    depth = -(-(2 * chunk + 1) // 8) * 8
    f32, bf16 = jnp.float32, jnp.bfloat16
    any_spec = pl.BlockSpec(memory_space=pl.ANY)
    vmem_spec = pl.BlockSpec(memory_space=pltpu.VMEM)
    dma = pltpu.SemaphoreType.DMA
    flops = 2 * chunk * c_out * c_in * cols
    projected = pl.pallas_call(
        functools.partial(kernel, n_rows, n),
        out_shape=jax.ShapeDtypeStruct((chunk, c_out, cols), bf16),
        in_specs=[any_spec, vmem_spec, vmem_spec, any_spec, any_spec],
        out_specs=any_spec,
        scratch_shapes=[
            pltpu.VMEM((n, chunk, ch, cols), bf16),
            pltpu.VMEM((n, chunk, ch, cols), bf16),
            pltpu.VMEM((c_out, c_in), bf16),
            pltpu.VMEM((3, n, chunk, cols), f32),
            pltpu.VMEM((n, chunk, cols), f32),
            pltpu.VMEM((n, depth, cols), f32),
            pltpu.VMEM((n + 1, cols, cols), bf16),
            pltpu.VMEM((n + 1, cols, cols), bf16),
            pltpu.VMEM((n, ch, cols), f32),
            pltpu.VMEM((ch, cols), f32),
            pltpu.VMEM((ch, cols), f32),
            pltpu.VMEM((ch, cols), f32),
            pltpu.VMEM((ch, cols), bf16),
            pltpu.VMEM((ch, cols), bf16),
            pltpu.VMEM((n, chunk, ch, cols), bf16),
            pltpu.VMEM((chunk, c_in, cols), bf16),
            pltpu.VMEM((chunk, c_out, cols), bf16),
            dma((n,)),
            dma((n,)),
            dma,
            dma((chunk,)),
            dma((chunk, n)),
            dma((chunk, n)),
            dma((tiles,)),
            dma((tiles,)),
        ],
        compiler_params=pltpu.CompilerParams(
            collective_id=0, has_side_effects=True, vmem_limit_bytes=58 * 2**20),
        cost_estimate=pl.CostEstimate(flops=flops, bytes_accessed=4 * features.size * 2, transcendentals=features.size),
    )(
        features.reshape(n, chunk, ch, cols),
        mixing.reshape(3, n, chunk, cols),
        decay_rate.reshape(n, chunk, cols),
        gate_input.reshape(n, chunk, ch, cols),
        out_weight,
    )
    return pl.pallas_call(
        copy_kernel,
        out_shape=jax.ShapeDtypeStruct(projected.shape, bf16),
        in_specs=[any_spec],
        out_specs=any_spec,
        scratch_shapes=[pltpu.VMEM(projected.shape, bf16), dma((chunk,)), dma((chunk,))],
        compiler_params=pltpu.CompilerParams(vmem_limit_bytes=58 * 2**20),
    )(projected)


def solution(mesh):
    n_rows, n = mesh.shape["rows"], mesh.shape["chan"]
    in_specs = (
        P("rows", "chan", None),
        P(None, "rows", None),
        P("rows", None),
        P("rows", "chan", None),
        P(),
    )
    out_specs = P(("rows", "chan"), None, None)
    return jax.shard_map(
        functools.partial(shards, n_rows, n), mesh=mesh, in_specs=in_specs, out_specs=out_specs, check_vma=False)
```

```python
import functools

import jax
import jax.numpy as jnp
from jax import lax
from jax.experimental import pallas as pl
from jax.experimental.pallas import tpu as pltpu
from jax.sharding import PartitionSpec as P

MESH = pl.DeviceIdType.MESH


def tile_of(size, choices):
    return next(t for t in choices if size % t == 0)


def halves(value):
    high = value.astype(jnp.bfloat16)
    return high, (value - high.astype(jnp.float32)).astype(jnp.bfloat16)


def dot3(a_hi, a_lo, b_hi, b_lo):
    dot = functools.partial(jnp.dot, preferred_element_type=jnp.float32)
    return dot(a_hi, b_hi) + (dot(a_hi, b_lo) + dot(a_lo, b_hi))


def partner(me, k, n):
    half = n // 2
    mask = jnp.where(k < half, n - 1 - k, (k - half + 1) % half)
    result, bit = 0, 1
    while bit < n:
        result += (me // bit + mask // bit) % 2 * bit
        bit *= 2
    return result


def kernel(n_rows, n, feat_hbm, mix_ref, decay_ref, gate_hbm, w_hbm, out_hbm,
           feat, gate, weight, coef, scale, band, ops_hi, ops_lo, starts, tail,
           incoming, outgoing, come_hi, come_lo, sent, got, result,
           feat_sem, gate_sem, weight_sem, out_sem, send_sem, recv_sem, relay_send, relay_recv):
    _, chunk, ch, cols = feat.shape
    c_out = weight.shape[0]
    p, me = lax.axis_index("rows"), lax.axis_index("chan")
    tile = tile_of(ch, (64, 48, 32, 16))
    tiles = ch // tile
    o_tile = tile_of(c_out, (256, 128, 64, 32, 16))

    def feat_copy(j):
        return pltpu.make_async_copy(feat_hbm.at[j], feat.at[j], feat_sem.at[j])

    def gate_copy(j):
        return pltpu.make_async_copy(gate_hbm.at[j], gate.at[j], gate_sem.at[j])

    weight_copy = pltpu.make_async_copy(w_hbm, weight, weight_sem)

    @pl.loop(0, n)
    def _(j):
        feat_copy(j).start()

    @pl.loop(0, n)
    def _(j):
        gate_copy(j).start()

    weight_copy.start()

    barrier = pltpu.get_barrier_semaphore()

    @pl.loop(0, n - 1)
    def _(k):
        pl.semaphore_signal(barrier, inc=1, device_id={"chan": partner(me, k, n)}, device_id_type=MESH)

    @pl.when(p > 0)
    def _():
        pl.semaphore_signal(barrier, inc=1, device_id={"rows": p - 1}, device_id_type=MESH)

    @pl.when(p < n_rows - 1)
    def _():
        pl.semaphore_signal(barrier, inc=1, device_id={"rows": p + 1}, device_id_type=MESH)

    retain = 1.0 - decay_ref[...]
    for s in range(3):
        coef[s] = retain * mix_ref[s]
    scale[...] = jnp.sqrt(decay_ref[...])

    def step(state, j, row):
        left_w = coef[0, j, pl.ds(row, 1), :]
        mid_w = coef[1, j, pl.ds(row, 1), :]
        right_w = coef[2, j, pl.ds(row, 1), :]
        return left_w * pltpu.roll(state, 1, 1) + mid_w * state + right_w * pltpu.roll(state, cols - 1, 1)

    def advance(state, j, row, at):
        push = scale[j, pl.ds(row, 1), :] * feat[j, row, at, :].astype(jnp.float32)
        return step(state, j, row) + push

    def scan_tile(j, t):
        at = pl.ds(t * tile, tile)
        state = tail[at, :]
        starts[j, at, :] = state
        for row in range(chunk):
            state = advance(state, j, row, at)
        tail[at, :] = state

    tail[...] = jnp.zeros_like(tail)

    @pl.when(p == 0)
    def _():
        @pl.loop(0, n)
        def _(j):
            feat_copy(j).wait()
            for t in range(tiles):
                scan_tile(j, t)

    @pl.when(p > 0)
    def _():
        depth = band.shape[1]
        diagonal = lax.broadcasted_iota(jnp.int32, band.shape, 1)
        value = jnp.where(diagonal == chunk, 1.0, 0.0).astype(jnp.float32)
        for row in range(chunk):
            below = pltpu.roll(pltpu.roll(value, depth - 1, 1), 1, 2)
            above = pltpu.roll(pltpu.roll(value, 1, 1), cols - 1, 2)
            value = (coef[0, :, row:row + 1, :] * below + coef[1, :, row:row + 1, :] * value
                     + coef[2, :, row:row + 1, :] * above)
        band[...] = value
        offset = (lax.broadcasted_iota(jnp.int32, (cols, cols), 0)
                  - lax.broadcasted_iota(jnp.int32, (cols, cols), 1))
        ops_hi[0] = jnp.where(offset == 0, 1.0, 0.0).astype(jnp.bfloat16)
        ops_lo[0] = jnp.zeros((cols, cols), jnp.bfloat16)

        @pl.loop(0, n)
        def _(j):
            feat_copy(j).wait()
            dense = jnp.zeros((cols, cols), jnp.float32)
            for k in range(2 * chunk + 1):
                dense = jnp.where(offset == k - chunk, band[j, k:k + 1, :], dense)
            product = dot3(ops_hi[j], ops_lo[j], *halves(dense))
            ops_hi[j + 1], ops_lo[j + 1] = halves(product)
            for t in range(tiles):
                scan_tile(j, t)

    pl.semaphore_wait(barrier, n - 1 + jnp.where(p > 0, 1, 0) + jnp.where(p < n_rows - 1, 1, 0))

    def relay(device, t):
        at = pl.ds(t * tile, tile)
        return pltpu.make_async_remote_copy(
            src_ref=outgoing.at[at, :], dst_ref=incoming.at[at, :],
            send_sem=relay_send.at[t], recv_sem=relay_recv.at[t],
            device_id={"rows": device}, device_id_type=MESH)

    for t in range(tiles):
        at = pl.ds(t * tile, tile)

        @pl.when(p > 0)
        def _():
            relay(p - 1, t).wait_recv()
            come_hi[at, :], come_lo[at, :] = halves(incoming[at, :])

        @pl.when(p < n_rows - 1)
        def _():
            @pl.when(p == 0)
            def _():
                outgoing[at, :] = tail[at, :]

            @pl.when(p > 0)
            def _():
                outgoing[at, :] = tail[at, :] + dot3(come_hi[at, :], come_lo[at, :], ops_hi[n], ops_lo[n])

            relay(p + 1, t).start()

    def send(row, k):
        return pltpu.make_async_remote_copy(
            src_ref=sent.at[k, row], dst_ref=got.at[row, pl.ds(pl.multiple_of(me * ch, ch), ch), :],
            send_sem=send_sem.at[row, k], recv_sem=recv_sem.at[row, k],
            device_id={"chan": partner(me, k, n)}, device_id_type=MESH)

    def gated_row(j, row, put):
        @pl.loop(0, tiles)
        def _(t):
            at = pl.ds(pl.multiple_of(t * tile, tile), tile)
            state = advance(starts[j, at, :], j, row, at)
            starts[j, at, :] = state
            v = gate[j, row, at, :].astype(jnp.float32)
            put(t, (state * (v / (1.0 + jnp.exp(-v)))).astype(jnp.bfloat16))

    def make_row(row):
        @pl.loop(0, n)
        def _(k):
            j = partner(me, k, n)

            @pl.when(row == 0)
            def _():
                gate_copy(j).wait()

                @pl.when(p > 0)
                def _():
                    starts[j] = starts[j] + dot3(come_hi[...], come_lo[...], ops_hi[j], ops_lo[j])

            @pl.when(k < n - 1)
            def _():
                def put(t, value):
                    sent[k, row, pl.ds(pl.multiple_of(t * tile, tile), tile), :] = value

                gated_row(j, row, put)
                send(row, k).start()

            @pl.when(k == n - 1)
            def _():
                def put(t, value):
                    got[row, pl.ds(pl.multiple_of(me * ch + t * tile, tile), tile), :] = value

                gated_row(j, row, put)

    def out_copy(row):
        return pltpu.make_async_copy(result.at[row], out_hbm.at[row], out_sem.at[row])

    def project_row(row):
        @pl.loop(0, n - 1)
        def _(k):
            send(row, k).wait_recv()

        @pl.loop(0, c_out // o_tile)
        def _(o):
            at = pl.ds(pl.multiple_of(o * o_tile, o_tile), o_tile)
            result[row, at, :] = jnp.dot(
                weight[at, :], got[row], preferred_element_type=jnp.float32).astype(jnp.bfloat16)

        out_copy(row).start()

    window = min(3, chunk)

    @pl.loop(0, chunk + window)
    def _(turn):
        @pl.when(turn >= window)
        def _():
            @pl.loop(0, n - 1)
            def _(k):
                send(turn - window, k).wait_send()

        @pl.when(turn < chunk)
        def _():
            make_row(turn)

        @pl.when(turn == window)
        def _():
            weight_copy.wait()

        @pl.when(turn >= window)
        def _():
            project_row(turn - window)

    @pl.loop(0, chunk)
    def _(row):
        out_copy(row).wait()

    @pl.when(p < n_rows - 1)
    def _():
        for t in range(tiles):
            relay(p + 1, t).wait_send()


def copy_kernel(source, target, held, in_sem, out_sem):
    rows = range(source.shape[0])
    ins = [pltpu.make_async_copy(source.at[i], held.at[i], in_sem.at[i]) for i in rows]
    outs = [pltpu.make_async_copy(held.at[i], target.at[i], out_sem.at[i]) for i in rows]
    for copy in ins:
        copy.start()
    for i in rows:
        ins[i].wait()
        outs[i].start()
    for copy in outs:
        copy.wait()


def shards(n_rows, n, features, mixing, decay_rate, gate_input, out_weight):
    rows_here, ch, cols = features.shape
    chunk = rows_here // n
    c_out, c_in = out_weight.shape
    tiles = ch // tile_of(ch, (64, 48, 32, 16))
    depth = -(-(2 * chunk + 1) // 8) * 8
    f32, bf16 = jnp.float32, jnp.bfloat16
    any_spec = pl.BlockSpec(memory_space=pl.ANY)
    vmem_spec = pl.BlockSpec(memory_space=pltpu.VMEM)
    dma = pltpu.SemaphoreType.DMA
    flops = 2 * chunk * c_out * c_in * cols
    projected = pl.pallas_call(
        functools.partial(kernel, n_rows, n),
        out_shape=jax.ShapeDtypeStruct((chunk, c_out, cols), bf16),
        in_specs=[any_spec, vmem_spec, vmem_spec, any_spec, any_spec],
        out_specs=any_spec,
        scratch_shapes=[
            pltpu.VMEM((n, chunk, ch, cols), bf16),
            pltpu.VMEM((n, chunk, ch, cols), bf16),
            pltpu.VMEM((c_out, c_in), bf16),
            pltpu.VMEM((3, n, chunk, cols), f32),
            pltpu.VMEM((n, chunk, cols), f32),
            pltpu.VMEM((n, depth, cols), f32),
            pltpu.VMEM((n + 1, cols, cols), bf16),
            pltpu.VMEM((n + 1, cols, cols), bf16),
            pltpu.VMEM((n, ch, cols), f32),
            pltpu.VMEM((ch, cols), f32),
            pltpu.VMEM((ch, cols), f32),
            pltpu.VMEM((ch, cols), f32),
            pltpu.VMEM((ch, cols), bf16),
            pltpu.VMEM((ch, cols), bf16),
            pltpu.VMEM((n, chunk, ch, cols), bf16),
            pltpu.VMEM((chunk, c_in, cols), bf16),
            pltpu.VMEM((chunk, c_out, cols), bf16),
            dma((n,)),
            dma((n,)),
            dma,
            dma((chunk,)),
            dma((chunk, n)),
            dma((chunk, n)),
            dma((tiles,)),
            dma((tiles,)),
        ],
        compiler_params=pltpu.CompilerParams(
            collective_id=0, has_side_effects=True, vmem_limit_bytes=58 * 2**20),
        cost_estimate=pl.CostEstimate(flops=flops, bytes_accessed=4 * features.size * 2, transcendentals=features.size),
    )(
        features.reshape(n, chunk, ch, cols),
        mixing.reshape(3, n, chunk, cols),
        decay_rate.reshape(n, chunk, cols),
        gate_input.reshape(n, chunk, ch, cols),
        out_weight,
    )
    return pl.pallas_call(
        copy_kernel,
        out_shape=jax.ShapeDtypeStruct(projected.shape, bf16),
        in_specs=[any_spec],
        out_specs=any_spec,
        scratch_shapes=[pltpu.VMEM(projected.shape, bf16), dma((chunk,)), dma((chunk,))],
        compiler_params=pltpu.CompilerParams(vmem_limit_bytes=58 * 2**20),
    )(projected)


def solution(mesh):
    n_rows, n = mesh.shape["rows"], mesh.shape["chan"]
    in_specs = (
        P("rows", "chan", None),
        P(None, "rows", None),
        P("rows", None),
        P("rows", "chan", None),
        P(),
    )
    out_specs = P(("rows", "chan"), None, None)
    return jax.shard_map(
        functools.partial(shards, n_rows, n), mesh=mesh, in_specs=in_specs, out_specs=out_specs, check_vma=False)
```

```python
import functools

import jax
import jax.numpy as jnp
from jax import lax
from jax.experimental import pallas as pl
from jax.experimental.pallas import tpu as pltpu
from jax.sharding import PartitionSpec as P

MESH = pl.DeviceIdType.MESH


def tile_of(size, choices):
    return next(t for t in choices if size % t == 0)


def halves(value):
    high = value.astype(jnp.bfloat16)
    return high, (value - high.astype(jnp.float32)).astype(jnp.bfloat16)


def dot3(a_hi, a_lo, b_hi, b_lo):
    dot = functools.partial(jnp.dot, preferred_element_type=jnp.float32)
    return dot(a_hi, b_hi) + (dot(a_hi, b_lo) + dot(a_lo, b_hi))


def partner(me, k, n):
    half = n // 2
    mask = jnp.where(k < half, n - 1 - k, (k - half + 1) % half)
    result, bit = 0, 1
    while bit < n:
        result += (me // bit + mask // bit) % 2 * bit
        bit *= 2
    return result


def kernel(n_rows, n, feat_hbm, mix_hbm, decay_hbm, gate_hbm, w_hbm, out_hbm,
           feat, gate, mix, decay, weight, coef, scale, band, ops_hi, ops_lo, starts, tail,
           incoming, outgoing, come_hi, come_lo, sent, got, result,
           feat_sem, gate_sem, mix_sem, decay_sem, weight_sem, out_sem, send_sem, recv_sem, relay_send, relay_recv):
    _, chunk, ch, cols = feat.shape
    c_out = weight.shape[0]
    p, me = lax.axis_index("rows"), lax.axis_index("chan")
    tile = tile_of(ch, (64, 48, 32, 16))
    tiles = ch // tile
    o_tile = tile_of(c_out, (256, 128, 64, 32, 16))

    def feat_copy(j):
        return pltpu.make_async_copy(feat_hbm.at[j], feat.at[j], feat_sem.at[j])

    def gate_copy(j):
        return pltpu.make_async_copy(gate_hbm.at[j], gate.at[j], gate_sem.at[j])

    weight_copy = pltpu.make_async_copy(w_hbm, weight, weight_sem)

    mix_copy = pltpu.make_async_copy(mix_hbm, mix, mix_sem)
    decay_copy = pltpu.make_async_copy(decay_hbm, decay, decay_sem)
    mix_copy.start()
    decay_copy.start()

    @pl.loop(0, n)
    def _(j):
        feat_copy(j).start()

    barrier = pltpu.get_barrier_semaphore()

    @pl.loop(0, n - 1)
    def _(k):
        pl.semaphore_signal(barrier, inc=1, device_id={"chan": partner(me, k, n)}, device_id_type=MESH)

    @pl.when(p > 0)
    def _():
        pl.semaphore_signal(barrier, inc=1, device_id={"rows": p - 1}, device_id_type=MESH)

    @pl.when(p < n_rows - 1)
    def _():
        pl.semaphore_signal(barrier, inc=1, device_id={"rows": p + 1}, device_id_type=MESH)

    mix_copy.wait()
    decay_copy.wait()
    retain = 1.0 - decay[...]
    for s in range(3):
        coef[s] = retain * mix[s]
    scale[...] = jnp.sqrt(decay[...])

    def step(state, j, row):
        left_w = coef[0, j, pl.ds(row, 1), :]
        mid_w = coef[1, j, pl.ds(row, 1), :]
        right_w = coef[2, j, pl.ds(row, 1), :]
        return left_w * pltpu.roll(state, 1, 1) + mid_w * state + right_w * pltpu.roll(state, cols - 1, 1)

    def advance(state, j, row, at):
        push = scale[j, pl.ds(row, 1), :] * feat[j, row, at, :].astype(jnp.float32)
        return step(state, j, row) + push

    def scan_tile(j, t):
        at = pl.ds(t * tile, tile)
        state = tail[at, :]
        starts[j, at, :] = state
        for row in range(chunk):
            state = advance(state, j, row, at)
        tail[at, :] = state

    tail[...] = jnp.zeros_like(tail)

    @pl.when(p == 0)
    def _():
        @pl.loop(0, n)
        def _(j):
            feat_copy(j).wait()
            gate_copy(partner(me, j, n)).start()
            for t in range(tiles):
                scan_tile(j, t)

    @pl.when(p > 0)
    def _():
        depth = band.shape[1]
        diagonal = lax.broadcasted_iota(jnp.int32, band.shape, 1)
        value = jnp.where(diagonal == chunk, 1.0, 0.0).astype(jnp.float32)
        for row in range(chunk):
            below = pltpu.roll(pltpu.roll(value, depth - 1, 1), 1, 2)
            above = pltpu.roll(pltpu.roll(value, 1, 1), cols - 1, 2)
            value = (coef[0, :, row:row + 1, :] * below + coef[1, :, row:row + 1, :] * value
                     + coef[2, :, row:row + 1, :] * above)
        band[...] = value
        offset = (lax.broadcasted_iota(jnp.int32, (cols, cols), 0)
                  - lax.broadcasted_iota(jnp.int32, (cols, cols), 1))
        half, edge = cols // 2, -(-chunk // 8) * 8

        def block(j, top, height, left):
            block_offset = offset[top:top + height, left:left + half]
            value = jnp.zeros((height, half), jnp.float32)
            for k in range(2 * chunk + 1):
                value = jnp.where(block_offset == k - chunk, band[j, k:k + 1, left:left + half], value)
            return value

        def dense_of(j):
            empty = jnp.zeros((half - edge, half), jnp.float32)
            upper = jnp.concatenate([empty, block(j, half - edge, edge, half)], axis=0)
            lower = jnp.concatenate([block(j, half, edge, 0), empty], axis=0)
            return jnp.concatenate([
                jnp.concatenate([block(j, 0, half, 0), upper], axis=1),
                jnp.concatenate([lower, block(j, half, half, half)], axis=1)], axis=0)

        ops_hi[0] = jnp.where(offset == 0, 1.0, 0.0).astype(jnp.bfloat16)
        ops_lo[0] = jnp.zeros((cols, cols), jnp.bfloat16)

        @pl.loop(0, n)
        def _(j):
            feat_copy(j).wait()
            gate_copy(partner(me, j, n)).start()
            product = dot3(ops_hi[j], ops_lo[j], *halves(dense_of(j)))
            ops_hi[j + 1], ops_lo[j + 1] = halves(product)
            for t in range(tiles):
                scan_tile(j, t)

    weight_copy.start()
    pl.semaphore_wait(barrier, n - 1 + jnp.where(p > 0, 1, 0) + jnp.where(p < n_rows - 1, 1, 0))

    def relay(device, t):
        at = pl.ds(t * tile, tile)
        return pltpu.make_async_remote_copy(
            src_ref=outgoing.at[at, :], dst_ref=incoming.at[at, :],
            send_sem=relay_send.at[t], recv_sem=relay_recv.at[t],
            device_id={"rows": device}, device_id_type=MESH)

    for t in range(tiles):
        at = pl.ds(t * tile, tile)

        @pl.when(p > 0)
        def _():
            relay(p - 1, t).wait_recv()
            come_hi[at, :], come_lo[at, :] = halves(incoming[at, :])

        @pl.when(p < n_rows - 1)
        def _():
            @pl.when(p == 0)
            def _():
                outgoing[at, :] = tail[at, :]

            @pl.when(p > 0)
            def _():
                outgoing[at, :] = tail[at, :] + dot3(come_hi[at, :], come_lo[at, :], ops_hi[n], ops_lo[n])

            relay(p + 1, t).start()

    def send(row, k):
        return pltpu.make_async_remote_copy(
            src_ref=sent.at[k, row], dst_ref=got.at[row, pl.ds(pl.multiple_of(me * ch, ch), ch), :],
            send_sem=send_sem.at[row, k], recv_sem=recv_sem.at[row, k],
            device_id={"chan": partner(me, k, n)}, device_id_type=MESH)

    def gated_row(j, row, put):
        @pl.loop(0, tiles)
        def _(t):
            at = pl.ds(pl.multiple_of(t * tile, tile), tile)
            state = advance(starts[j, at, :], j, row, at)
            starts[j, at, :] = state
            v = gate[j, row, at, :].astype(jnp.float32)
            put(t, (state * (v / (1.0 + jnp.exp(-v)))).astype(jnp.bfloat16))

    @pl.loop(0, chunk)
    def _(row):
        @pl.loop(0, n)
        def _(k):
            j = partner(me, k, n)

            @pl.when(row == 0)
            def _():
                gate_copy(j).wait()

                @pl.when(p > 0)
                def _():
                    starts[j] = starts[j] + dot3(come_hi[...], come_lo[...], ops_hi[j], ops_lo[j])

            @pl.when(k < n - 1)
            def _():
                def put(t, value):
                    sent[k, row, pl.ds(pl.multiple_of(t * tile, tile), tile), :] = value

                gated_row(j, row, put)
                send(row, k).start()

            @pl.when(k == n - 1)
            def _():
                def put(t, value):
                    got[row, pl.ds(pl.multiple_of(me * ch + t * tile, tile), tile), :] = value

                gated_row(j, row, put)

    weight_copy.wait()

    def out_copy(row):
        return pltpu.make_async_copy(result.at[row], out_hbm.at[row], out_sem.at[row])

    @pl.loop(0, chunk)
    def _(row):
        @pl.loop(0, n - 1)
        def _(k):
            send(row, k).wait_recv()

        @pl.loop(0, c_out // o_tile)
        def _(o):
            at = pl.ds(pl.multiple_of(o * o_tile, o_tile), o_tile)
            result[row, at, :] = jnp.dot(
                weight[at, :], got[row], preferred_element_type=jnp.float32).astype(jnp.bfloat16)

        out_copy(row).start()

    @pl.loop(0, chunk)
    def _(row):
        @pl.loop(0, n - 1)
        def _(k):
            send(row, k).wait_send()

        out_copy(row).wait()

    @pl.when(p < n_rows - 1)
    def _():
        for t in range(tiles):
            relay(p + 1, t).wait_send()


def copy_kernel(source, target, held, in_sem, out_sem):
    rows = range(source.shape[0])
    ins = [pltpu.make_async_copy(source.at[i], held.at[i], in_sem.at[i]) for i in rows]
    outs = [pltpu.make_async_copy(held.at[i], target.at[i], out_sem.at[i]) for i in rows]
    for copy in ins:
        copy.start()
    for i in rows:
        ins[i].wait()
        outs[i].start()
    for copy in outs:
        copy.wait()


def shards(n_rows, n, features, mixing, decay_rate, gate_input, out_weight):
    rows_here, ch, cols = features.shape
    chunk = rows_here // n
    c_out, c_in = out_weight.shape
    tiles = ch // tile_of(ch, (64, 48, 32, 16))
    depth = -(-(2 * chunk + 1) // 8) * 8
    f32, bf16 = jnp.float32, jnp.bfloat16
    any_spec = pl.BlockSpec(memory_space=pl.ANY)
    dma = pltpu.SemaphoreType.DMA
    flops = 2 * chunk * c_out * c_in * cols
    projected = pl.pallas_call(
        functools.partial(kernel, n_rows, n),
        out_shape=jax.ShapeDtypeStruct((chunk, c_out, cols), bf16),
        in_specs=[any_spec] * 5,
        out_specs=any_spec,
        scratch_shapes=[
            pltpu.VMEM((n, chunk, ch, cols), bf16),
            pltpu.VMEM((n, chunk, ch, cols), bf16),
            pltpu.VMEM((3, n, chunk, cols), f32),
            pltpu.VMEM((n, chunk, cols), f32),
            pltpu.VMEM((c_out, c_in), bf16),
            pltpu.VMEM((3, n, chunk, cols), f32),
            pltpu.VMEM((n, chunk, cols), f32),
            pltpu.VMEM((n, depth, cols), f32),
            pltpu.VMEM((n + 1, cols, cols), bf16),
            pltpu.VMEM((n + 1, cols, cols), bf16),
            pltpu.VMEM((n, ch, cols), f32),
            pltpu.VMEM((ch, cols), f32),
            pltpu.VMEM((ch, cols), f32),
            pltpu.VMEM((ch, cols), f32),
            pltpu.VMEM((ch, cols), bf16),
            pltpu.VMEM((ch, cols), bf16),
            pltpu.VMEM((n, chunk, ch, cols), bf16),
            pltpu.VMEM((chunk, c_in, cols), bf16),
            pltpu.VMEM((chunk, c_out, cols), bf16),
            dma((n,)),
            dma((n,)),
            dma,
            dma,
            dma,
            dma((chunk,)),
            dma((chunk, n)),
            dma((chunk, n)),
            dma((tiles,)),
            dma((tiles,)),
        ],
        compiler_params=pltpu.CompilerParams(
            collective_id=0, has_side_effects=True, vmem_limit_bytes=58 * 2**20),
        cost_estimate=pl.CostEstimate(flops=flops, bytes_accessed=4 * features.size * 2, transcendentals=features.size),
    )(
        features.reshape(n, chunk, ch, cols),
        mixing.reshape(3, n, chunk, cols),
        decay_rate.reshape(n, chunk, cols),
        gate_input.reshape(n, chunk, ch, cols),
        out_weight,
    )
    return pl.pallas_call(
        copy_kernel,
        out_shape=jax.ShapeDtypeStruct(projected.shape, bf16),
        in_specs=[any_spec],
        out_specs=any_spec,
        scratch_shapes=[pltpu.VMEM(projected.shape, bf16), dma((chunk,)), dma((chunk,))],
        compiler_params=pltpu.CompilerParams(vmem_limit_bytes=58 * 2**20),
    )(projected)


def solution(mesh):
    n_rows, n = mesh.shape["rows"], mesh.shape["chan"]
    in_specs = (
        P("rows", "chan", None),
        P(None, "rows", None),
        P("rows", None),
        P("rows", "chan", None),
        P(),
    )
    out_specs = P(("rows", "chan"), None, None)
    return jax.shard_map(
        functools.partial(shards, n_rows, n), mesh=mesh, in_specs=in_specs, out_specs=out_specs, check_vma=False)
```

```python
import functools

import jax
import jax.numpy as jnp
from jax import lax
from jax.experimental import pallas as pl
from jax.experimental.pallas import tpu as pltpu
from jax.sharding import PartitionSpec as P

MESH = pl.DeviceIdType.MESH


def tile_of(size, choices):
    return next(t for t in choices if size % t == 0)


def halves(value):
    high = value.astype(jnp.bfloat16)
    return high, (value - high.astype(jnp.float32)).astype(jnp.bfloat16)


def dot3(a_hi, a_lo, b_hi, b_lo):
    dot = functools.partial(jnp.dot, preferred_element_type=jnp.float32)
    return dot(a_hi, b_hi) + (dot(a_hi, b_lo) + dot(a_lo, b_hi))


def partner(me, k, n):
    half = n // 2
    mask = jnp.where(k < half, n - 1 - k, (k - half + 1) % half)
    result, bit = 0, 1
    while bit < n:
        result += (me // bit + mask // bit) % 2 * bit
        bit *= 2
    return result


def kernel(n_rows, n, feat_hbm, mix_hbm, decay_hbm, gate_hbm, w_hbm, out_hbm,
           feat, gate, mix, decay, weight, coef, scale, band, ops_hi, ops_lo, starts, tail,
           incoming, outgoing, come_hi, come_lo, sent, got, result,
           feat_sem, gate_sem, mix_sem, decay_sem, weight_sem, out_sem, send_sem, recv_sem, relay_send, relay_recv):
    _, chunk, ch, cols = feat.shape
    c_out = weight.shape[0]
    p, me = lax.axis_index("rows"), lax.axis_index("chan")
    tile = tile_of(ch, (64, 48, 32, 16))
    tiles = ch // tile
    o_tile = tile_of(c_out, (256, 128, 64, 32, 16))

    def feat_copy(j):
        return pltpu.make_async_copy(feat_hbm.at[j], feat.at[j], feat_sem.at[j])

    def gate_copy(j):
        return pltpu.make_async_copy(gate_hbm.at[j], gate.at[j], gate_sem.at[j])

    weight_copy = pltpu.make_async_copy(w_hbm, weight, weight_sem)

    mix_copy = pltpu.make_async_copy(mix_hbm, mix, mix_sem)
    decay_copy = pltpu.make_async_copy(decay_hbm, decay, decay_sem)
    mix_copy.start()
    decay_copy.start()

    @pl.loop(0, n)
    def _(j):
        feat_copy(j).start()

    barrier = pltpu.get_barrier_semaphore()

    @pl.loop(0, n - 1)
    def _(k):
        pl.semaphore_signal(barrier, inc=1, device_id={"chan": partner(me, k, n)}, device_id_type=MESH)

    @pl.when(p > 0)
    def _():
        pl.semaphore_signal(barrier, inc=1, device_id={"rows": p - 1}, device_id_type=MESH)

    @pl.when(p < n_rows - 1)
    def _():
        pl.semaphore_signal(barrier, inc=1, device_id={"rows": p + 1}, device_id_type=MESH)

    mix_copy.wait()
    decay_copy.wait()
    retain = 1.0 - decay[...]
    for s in range(3):
        coef[s] = retain * mix[s]
    scale[...] = jnp.sqrt(decay[...])

    def step(state, j, row):
        left_w = coef[0, j, pl.ds(row, 1), :]
        mid_w = coef[1, j, pl.ds(row, 1), :]
        right_w = coef[2, j, pl.ds(row, 1), :]
        return left_w * pltpu.roll(state, 1, 1) + mid_w * state + right_w * pltpu.roll(state, cols - 1, 1)

    def advance(state, j, row, at):
        push = scale[j, pl.ds(row, 1), :] * feat[j, row, at, :].astype(jnp.float32)
        return step(state, j, row) + push

    def scan_tile(j, t):
        at = pl.ds(t * tile, tile)
        state = tail[at, :]
        starts[j, at, :] = state
        for row in range(chunk):
            state = advance(state, j, row, at)
        tail[at, :] = state

    tail[...] = jnp.zeros_like(tail)

    @pl.when(p == 0)
    def _():
        @pl.loop(0, n)
        def _(j):
            feat_copy(j).wait()
            gate_copy(partner(me, j, n)).start()
            for t in range(tiles):
                scan_tile(j, t)

    @pl.when(p > 0)
    def _():
        depth = band.shape[1]
        diagonal = lax.broadcasted_iota(jnp.int32, band.shape, 1)
        value = jnp.where(diagonal == chunk, 1.0, 0.0).astype(jnp.float32)
        for row in range(chunk):
            below = pltpu.roll(pltpu.roll(value, depth - 1, 1), 1, 2)
            above = pltpu.roll(pltpu.roll(value, 1, 1), cols - 1, 2)
            value = (coef[0, :, row:row + 1, :] * below + coef[1, :, row:row + 1, :] * value
                     + coef[2, :, row:row + 1, :] * above)
        band[...] = value
        offset = (lax.broadcasted_iota(jnp.int32, (cols, cols), 0)
                  - lax.broadcasted_iota(jnp.int32, (cols, cols), 1))
        half, edge = cols // 2, -(-chunk // 8) * 8

        def block(j, top, height, left):
            block_offset = offset[top:top + height, left:left + half]
            value = jnp.zeros((height, half), jnp.float32)
            for k in range(2 * chunk + 1):
                value = jnp.where(block_offset == k - chunk, band[j, k:k + 1, left:left + half], value)
            return value

        def dense_of(j):
            empty = jnp.zeros((half - edge, half), jnp.float32)
            upper = jnp.concatenate([empty, block(j, half - edge, edge, half)], axis=0)
            lower = jnp.concatenate([block(j, half, edge, 0), empty], axis=0)
            return jnp.concatenate([
                jnp.concatenate([block(j, 0, half, 0), upper], axis=1),
                jnp.concatenate([lower, block(j, half, half, half)], axis=1)], axis=0)

        ops_hi[0] = jnp.where(offset == 0, 1.0, 0.0).astype(jnp.bfloat16)
        ops_lo[0] = jnp.zeros((cols, cols), jnp.bfloat16)

        @pl.loop(0, n)
        def _(j):
            feat_copy(j).wait()
            gate_copy(partner(me, j, n)).start()
            product = dot3(ops_hi[j], ops_lo[j], *halves(dense_of(j)))
            ops_hi[j + 1], ops_lo[j + 1] = halves(product)
            for t in range(tiles):
                scan_tile(j, t)

    weight_copy.start()
    pl.semaphore_wait(barrier, n - 1 + jnp.where(p > 0, 1, 0) + jnp.where(p < n_rows - 1, 1, 0))

    def relay(device, t):
        at = pl.ds(t * tile, tile)
        return pltpu.make_async_remote_copy(
            src_ref=outgoing.at[at, :], dst_ref=incoming.at[at, :],
            send_sem=relay_send.at[t], recv_sem=relay_recv.at[t],
            device_id={"rows": device}, device_id_type=MESH)

    for t in range(tiles):
        at = pl.ds(t * tile, tile)

        @pl.when(p > 0)
        def _():
            relay(p - 1, t).wait_recv()
            come_hi[at, :], come_lo[at, :] = halves(incoming[at, :])

        @pl.when(p < n_rows - 1)
        def _():
            @pl.when(p == 0)
            def _():
                outgoing[at, :] = tail[at, :]

            @pl.when(p > 0)
            def _():
                outgoing[at, :] = tail[at, :] + dot3(come_hi[at, :], come_lo[at, :], ops_hi[n], ops_lo[n])

            relay(p + 1, t).start()

    def send(row, k):
        return pltpu.make_async_remote_copy(
            src_ref=sent.at[k, row], dst_ref=got.at[row, pl.ds(pl.multiple_of(me * ch, ch), ch), :],
            send_sem=send_sem.at[row, k], recv_sem=recv_sem.at[row, k],
            device_id={"chan": partner(me, k, n)}, device_id_type=MESH)

    def gated_row(j, row, put):
        @pl.loop(0, tiles)
        def _(t):
            at = pl.ds(pl.multiple_of(t * tile, tile), tile)
            state = advance(starts[j, at, :], j, row, at)
            starts[j, at, :] = state
            v = gate[j, row, at, :].astype(jnp.float32)
            put(t, (state * (v / (1.0 + jnp.exp(-v)))).astype(jnp.bfloat16))

    @pl.loop(0, chunk)
    def _(row):
        @pl.loop(0, n)
        def _(turn):
            k = jnp.where((row == chunk - 1) & (turn < n - 1), (turn + n // 2) % (n - 1), turn)
            j = partner(me, k, n)

            @pl.when(row == 0)
            def _():
                gate_copy(j).wait()

                @pl.when(p > 0)
                def _():
                    starts[j] = starts[j] + dot3(come_hi[...], come_lo[...], ops_hi[j], ops_lo[j])

            @pl.when(k < n - 1)
            def _():
                def put(t, value):
                    sent[k, row, pl.ds(pl.multiple_of(t * tile, tile), tile), :] = value

                gated_row(j, row, put)
                send(row, k).start()

            @pl.when(k == n - 1)
            def _():
                def put(t, value):
                    got[row, pl.ds(pl.multiple_of(me * ch + t * tile, tile), tile), :] = value

                gated_row(j, row, put)

    weight_copy.wait()

    def out_copy(row):
        return pltpu.make_async_copy(result.at[row], out_hbm.at[row], out_sem.at[row])

    @pl.loop(0, chunk)
    def _(row):
        @pl.loop(0, n - 1)
        def _(k):
            send(row, k).wait_recv()

        @pl.loop(0, c_out // o_tile)
        def _(o):
            at = pl.ds(pl.multiple_of(o * o_tile, o_tile), o_tile)
            result[row, at, :] = jnp.dot(
                weight[at, :], got[row], preferred_element_type=jnp.float32).astype(jnp.bfloat16)

        out_copy(row).start()

    @pl.loop(0, chunk)
    def _(row):
        @pl.loop(0, n - 1)
        def _(k):
            send(row, k).wait_send()

        out_copy(row).wait()

    @pl.when(p < n_rows - 1)
    def _():
        for t in range(tiles):
            relay(p + 1, t).wait_send()


def copy_kernel(source, target, held, in_sem, out_sem):
    rows = range(source.shape[0])
    ins = [pltpu.make_async_copy(source.at[i], held.at[i], in_sem.at[i]) for i in rows]
    outs = [pltpu.make_async_copy(held.at[i], target.at[i], out_sem.at[i]) for i in rows]
    for copy in ins[:3]:
        copy.start()
    for i in rows:
        ins[i].wait()
        outs[i].start()
        for copy in ins[i + 3:i + 4]:
            copy.start()
    for copy in outs:
        copy.wait()


def shards(n_rows, n, features, mixing, decay_rate, gate_input, out_weight):
    rows_here, ch, cols = features.shape
    chunk = rows_here // n
    c_out, c_in = out_weight.shape
    tiles = ch // tile_of(ch, (64, 48, 32, 16))
    depth = -(-(2 * chunk + 1) // 8) * 8
    f32, bf16 = jnp.float32, jnp.bfloat16
    any_spec = pl.BlockSpec(memory_space=pl.ANY)
    dma = pltpu.SemaphoreType.DMA
    flops = 2 * chunk * c_out * c_in * cols
    projected = pl.pallas_call(
        functools.partial(kernel, n_rows, n),
        out_shape=jax.ShapeDtypeStruct((chunk, c_out, cols), bf16),
        in_specs=[any_spec] * 5,
        out_specs=any_spec,
        scratch_shapes=[
            pltpu.VMEM((n, chunk, ch, cols), bf16),
            pltpu.VMEM((n, chunk, ch, cols), bf16),
            pltpu.VMEM((3, n, chunk, cols), f32),
            pltpu.VMEM((n, chunk, cols), f32),
            pltpu.VMEM((c_out, c_in), bf16),
            pltpu.VMEM((3, n, chunk, cols), f32),
            pltpu.VMEM((n, chunk, cols), f32),
            pltpu.VMEM((n, depth, cols), f32),
            pltpu.VMEM((n + 1, cols, cols), bf16),
            pltpu.VMEM((n + 1, cols, cols), bf16),
            pltpu.VMEM((n, ch, cols), f32),
            pltpu.VMEM((ch, cols), f32),
            pltpu.VMEM((ch, cols), f32),
            pltpu.VMEM((ch, cols), f32),
            pltpu.VMEM((ch, cols), bf16),
            pltpu.VMEM((ch, cols), bf16),
            pltpu.VMEM((n, chunk, ch, cols), bf16),
            pltpu.VMEM((chunk, c_in, cols), bf16),
            pltpu.VMEM((chunk, c_out, cols), bf16),
            dma((n,)),
            dma((n,)),
            dma,
            dma,
            dma,
            dma((chunk,)),
            dma((chunk, n)),
            dma((chunk, n)),
            dma((tiles,)),
            dma((tiles,)),
        ],
        compiler_params=pltpu.CompilerParams(
            collective_id=0, has_side_effects=True, vmem_limit_bytes=58 * 2**20),
        cost_estimate=pl.CostEstimate(flops=flops, bytes_accessed=4 * features.size * 2, transcendentals=features.size),
    )(
        features.reshape(n, chunk, ch, cols),
        mixing.reshape(3, n, chunk, cols),
        decay_rate.reshape(n, chunk, cols),
        gate_input.reshape(n, chunk, ch, cols),
        out_weight,
    )
    return pl.pallas_call(
        copy_kernel,
        out_shape=jax.ShapeDtypeStruct(projected.shape, bf16),
        in_specs=[any_spec],
        out_specs=any_spec,
        scratch_shapes=[pltpu.VMEM(projected.shape, bf16), dma((chunk,)), dma((chunk,))],
        compiler_params=pltpu.CompilerParams(vmem_limit_bytes=58 * 2**20),
    )(projected)


def solution(mesh):
    n_rows, n = mesh.shape["rows"], mesh.shape["chan"]
    in_specs = (
        P("rows", "chan", None),
        P(None, "rows", None),
        P("rows", None),
        P("rows", "chan", None),
        P(),
    )
    out_specs = P(("rows", "chan"), None, None)
    return jax.shard_map(
        functools.partial(shards, n_rows, n), mesh=mesh, in_specs=in_specs, out_specs=out_specs, check_vma=False)
```
